32 devices in a mesh: grp: 4 (over y, x), ta: 8 (over z, core).
Axes of the slice: x: 2, y: 2, z: 4, core: 2. Of those that a mesh axis runs over, the one named last changes fastest.
Arguments:
- gain: float32 [4096, 128, 128], P(('grp', 'ta')), as said below
- pred_mean: float32 [4096, 128], P(('grp', 'ta')), may hold values from -6 to 6
- update: float32 [4096, 128], P(('grp', 'ta')), as said below
- present: int32 [4096], P(('grp', 'ta')), may hold values 0 or 1
- step_cov: float32 [4096, 128, 128], P(('grp', 'ta')), as said below
Outputs:
- smooth_mean: float32 [4096, 128], P(('grp', 'ta'))
- smooth_cov: float32 [4096, 128, 128], P(('grp', 'ta'))
The draws below stay inside these ranges and needn't reach their ends.
Inputs may be any that keep to these rules, and one draw needn't show every extreme that they name: gain is a dense real matrix per step. `update`: any real values. `step_cov`: each step_cov_k is symmetric positive definite.
All inputs are finite; a program needn't handle non-finite values. No bound on the sum of `present` on one device may be relied on, other than what follows from the above.
Results may differ from the reference program's by a relative error of at most 0.0003.
Values sent between devices are 32-bit elements; how exact they have to be, the bound alone decides.
A program may use at most 128 MiB of HBM per device.

```python
import jax
import jax.numpy as jnp
from jax import lax

D = 128
STEPS = 4096


def channel_rates(key, share):
    key = jax.random.fold_in(key, 101)
    pick_key, slow_key, fast_key = jax.random.split(key, 3)
    picked = jax.random.uniform(pick_key, (D,)) < share
    slow = jnp.exp(jax.random.uniform(slow_key, (D,), minval=jnp.log(0.3), maxval=jnp.log(2.0))) / STEPS
    fast = jax.random.uniform(fast_key, (D,), minval=1.0 / 50.0, maxval=1.0 / 30.0)
    return jnp.where(picked, slow, fast)


def draw_gain(key, part):
    rates = channel_rates(key, 0.5)
    key = jax.random.fold_in(key, 1)
    hit_key, drop_key, noise_key = jax.random.split(key, 3)
    spread = 0.022 / jnp.sqrt(float(D))
    base = jnp.exp(-rates - D * spread * spread / 2.0)
    hits = jax.random.uniform(hit_key, (STEPS, D)) < 4.0 / STEPS
    drops = jax.random.uniform(drop_key, (STEPS, D), minval=0.5, maxval=0.8)
    diagonal = base[None, :] * jnp.where(hits, drops, 1.0)
    noise = jax.random.normal(noise_key, (STEPS, D, D)) * spread
    unit = jnp.eye(D, dtype=jnp.float32)
    return (noise * (1.0 - unit) + diagonal[:, :, None] * unit).astype(jnp.float32)


def draw_update(key, part):
    rates = channel_rates(key, 0.5)
    key = jax.random.fold_in(key, 2)
    values = jax.random.normal(key, (STEPS, D))
    return (values * jnp.sqrt(2.0 * rates)[None, :]).astype(jnp.float32)


def draw_step_cov(key, part):
    rates = channel_rates(key, 0.5)
    key = jax.random.fold_in(key, 3)
    sym_key, diag_key, step_key = jax.random.split(key, 3)
    raw = jax.random.normal(sym_key, (STEPS, D, D))
    coupling = (raw + jnp.swapaxes(raw, 1, 2)) * (0.25 / D)
    diagonal = jnp.exp(jax.random.uniform(diag_key, (STEPS, D), minval=0.0, maxval=jnp.log(4.0)))
    factor = jnp.exp(jax.random.uniform(step_key, (STEPS,), minval=jnp.log(0.5), maxval=jnp.log(2.0)))
    unit = jnp.eye(D, dtype=jnp.float32)
    core = coupling * (1.0 - unit) + diagonal[:, :, None] * unit
    root = jnp.sqrt(2.0 * rates)
    return (core * root[None, :, None] * root[None, None, :] * factor[:, None, None]).astype(jnp.float32)


def with_ends(result, own_key, low, high):
    spot = [jax.random.randint(jax.random.fold_in(own_key, axis), (), 0, length) for axis, length in enumerate(result.shape)]
    widest = result.shape.index(max(result.shape))
    neighbour = spot[:widest] + [(spot[widest] + 1) % result.shape[widest]] + spot[widest + 1:]
    return result.at[tuple(spot)].set(low).at[tuple(neighbour)].set(high)


def steps_of(stream_key, extent, cuts, least, high):
    def one(position, parts):
        steps = jax.random.uniform(jax.random.fold_in(jax.random.fold_in(stream_key, 6), position), (parts,), jnp.float32, least / len(cuts), high / len(cuts))
        return jnp.repeat(jnp.exp(steps), extent[position] // parts).reshape((-1,) + (1,) * (len(extent) - position - 1))

    loudness = one(*cuts[0])
    for cut in cuts[1:]:
        loudness = loudness * one(*cut)
    return loudness


def centred(own_key, extent, scale, reach, pieces=(), kind=jnp.bfloat16):
    level = steps_of(own_key, extent, pieces, -0.22, 0.18) if pieces else 1.0
    values = jax.random.normal(own_key, extent, jnp.float32) * scale * level
    return jnp.minimum(jnp.maximum(values, -reach), reach).astype(kind)


def setup_inputs(seed: int = 0) -> dict:
    seeds = jax.random.split(jax.random.key(seed), 6)
    gain = draw_gain(jax.random.fold_in(seeds[5], 71), 0)
    pred_mean = centred(seeds[1], (STEPS, D), 1.0, 6.0, ((0, 32),), jnp.float32)
    update = draw_update(jax.random.fold_in(seeds[5], 71), 0)
    present = with_ends((jax.random.randint(seeds[3], (STEPS,), 0, 4) < 3).astype(jnp.int32), jax.random.fold_in(seeds[3], 1), 0, 1)
    step_cov = draw_step_cov(jax.random.fold_in(seeds[5], 71), 0)
    return dict(gain=gain, pred_mean=pred_mean, update=update, present=present, step_cov=step_cov)


def reference(gain, pred_mean, update, present, step_cov):
    exact_mode = lax.Precision.HIGHEST
    gain_used = gain.at[-1].set(0.0)
    ahead = jnp.concatenate([pred_mean[1:], jnp.zeros((1, D), jnp.float32)], axis=0)
    filtered = pred_mean + present[:, None].astype(jnp.float32) * update
    offset = filtered - jnp.einsum("kij,kj->ki", gain_used, ahead, precision=exact_mode)

    def backward(state, element):
        mean_now, cov_now = state
        gain_step, offset_step, cov_step = element
        mean_new = jnp.dot(gain_step, mean_now, precision=exact_mode) + offset_step
        cov_new = jnp.dot(jnp.dot(gain_step, cov_now, precision=exact_mode), gain_step.T, precision=exact_mode) + cov_step
        return (mean_new, cov_new), (mean_new, cov_new)

    start = (jnp.zeros((D,), jnp.float32), jnp.zeros((D, D), jnp.float32))
    unused, outputs = lax.scan(backward, start, (gain_used, offset, step_cov), reverse=True)
    return (outputs[0], outputs[1])
```

```python
import functools

import jax
import jax.numpy as jnp
from jax import lax
from jax.experimental import pallas as pl
from jax.experimental.pallas import tpu as pltpu
from jax.sharding import PartitionSpec as P

AXES = ("grp", "ta")
CHAINS = 8
PAD = 16
F32, BF16 = jnp.float32, jnp.bfloat16


def halves(x):
    high = x.astype(BF16)
    low = (x - high.astype(F32)).astype(BF16)
    return high, low


def packed(x):
    return jnp.concatenate(halves(x), axis=1)


def weight_nt(g):
    high, low = halves(g)
    return jnp.concatenate(
        [jnp.concatenate([high, high], axis=1), jnp.concatenate([low, low], axis=1)], axis=0
    )


def weight_nn(g):
    row = packed(g)
    return jnp.concatenate([row, row], axis=0)


def diagonal_apart(g):
    on = lax.broadcasted_iota(jnp.int32, g.shape, 0) == lax.broadcasted_iota(jnp.int32, g.shape, 1)
    return jnp.sum(jnp.where(on, g, 0.0), axis=0, keepdims=True), jnp.where(on, 0.0, g)


def mul(x, w, dim, diagonal):
    out = lax.dot_general(packed(x), w, (((1,), (dim,)), ((), ())), preferred_element_type=F32)
    width = out.shape[1] // 2
    return out[:, :width] + out[:, width:] + x * diagonal


def advance(x, g, dim, lead, cov, extra):
    width = cov.shape[0]
    diagonal, rest = diagonal_apart(g)
    w = weight_nt(rest) if dim else weight_nn(rest)
    y = mul(x, w, dim, diagonal)
    turned = y[lead : lead + width].T
    return y[:lead], mul(turned, w, dim, diagonal) + cov, y[lead + width :] + extra


def measured(pres_ref, upd_ref, row):
    here = pres_ref[row].astype(F32) * upd_ref[pl.ds(row, 1), :]
    return jnp.broadcast_to(here, (PAD, here.shape[1]))


def is_last():
    length = lax.axis_size("ta")
    at = lax.axis_index("grp") * length + lax.axis_index("ta")
    return at == lax.axis_size("grp") * length - 1


def summary_kernel(pres_ref, g_ref, q_ref, upd_ref, out_ref):
    t = pl.program_id(0)
    chains, length = CHAINS, pl.num_programs(0)
    width = g_ref.shape[-1]
    s = length - 1 - t
    keep = jnp.where(is_last(), 0.0, 1.0).astype(F32)

    @pl.when(t == 0)
    def _():
        for b in range(chains):
            g = g_ref[b, 0]
            if b == chains - 1:
                g = g * keep
            out_ref[b, :width] = g.T
            out_ref[b, width : 2 * width] = q_ref[b, 0]
            out_ref[b, 2 * width :] = measured(pres_ref, upd_ref, b * length + s)

    @pl.when(t > 0)
    def _():
        for b in range(chains):
            g = g_ref[b, 0]
            extra = measured(pres_ref, upd_ref, b * length + s)
            lead, cov, d = advance(out_ref[b], g, 1, width, q_ref[b, 0], extra)
            out_ref[b, :width] = lead
            out_ref[b, width : 2 * width] = cov
            out_ref[b, 2 * width :] = d

    @pl.when(t == length - 1)
    def _():
        half = 1
        while half < chains:
            for first in range(0, chains, 2 * half):
                later = out_ref[first + half]
                for i in range(first, first + half):
                    own = out_ref[i]
                    lead, cov, d = advance(
                        later, own[:width], 0, width, own[width : 2 * width], own[2 * width :]
                    )
                    out_ref[i, :width] = lead
                    out_ref[i, width : 2 * width] = cov
                    out_ref[i, 2 * width :] = d
            half *= 2


def apply_kernel(pres_ref, g_ref, q_ref, upd_ref, pm_ref, suffix_ref, carry_ref, mean_ref, cov_ref, state):
    t = pl.program_id(0)
    chains, length = CHAINS, pl.num_programs(0)
    width = g_ref.shape[-1]
    s = length - 1 - t

    @pl.when(t == 0)
    def _():
        state[chains - 1] = jnp.where(is_last(), 0.0, carry_ref[...])
        for b in range(chains - 1):
            own = suffix_ref[b + 1]
            unused, cov, d = advance(
                carry_ref[...], own[:width], 0, 0, own[width : 2 * width], own[2 * width :]
            )
            state[b, :width] = cov
            state[b, width:] = d

    for b in range(chains):
        g = g_ref[b, 0]
        if b == chains - 1:
            g = g * jnp.where(is_last() & (t == 0), 0.0, 1.0).astype(F32)
        row = b * length + s
        unused, cov, d = advance(
            state[b], g, 1, 0, q_ref[b, 0], measured(pres_ref, upd_ref, row)
        )
        state[b, :width] = cov
        state[b, width:] = d
        cov_ref[b, 0] = cov
        mean_ref[pl.ds(row, 1), :] = pm_ref[pl.ds(row, 1), :] + d[:1]


def compose(own, later, width):
    exact = lax.Precision.HIGHEST
    turned = own[:width]
    y = jnp.matmul(later, turned, precision=exact)
    cov = jnp.matmul(y[width : 2 * width].T, turned, precision=exact) + own[width : 2 * width]
    return jnp.concatenate([y[:width], cov, y[2 * width :] + own[2 * width :]])


def moved(x, by):
    size = lax.axis_size(AXES)
    return lax.ppermute(x, AXES, [(i + by, i) for i in range(size - by)])


def body(gain, pred_mean, update, present, step_cov):
    steps, width = pred_mean.shape
    length = steps // CHAINS
    rows = 2 * width + PAD
    gain = gain.reshape(CHAINS, length, width, width)
    step_cov = step_cov.reshape(CHAINS, length, width, width)
    smem = pl.BlockSpec(memory_space=pltpu.SMEM)
    stream = pl.BlockSpec((CHAINS, 1, width, width), lambda t: (0, length - 1 - t, 0, 0))

    def fixed(*shape):
        return pl.BlockSpec(shape, lambda t: (0,) * len(shape))

    suffix = pl.pallas_call(
        summary_kernel,
        grid=(length,),
        in_specs=[smem, stream, stream, fixed(steps, width)],
        out_specs=fixed(CHAINS, rows, width),
        out_shape=jax.ShapeDtypeStruct((CHAINS, rows, width), F32),
        compiler_params=pltpu.CompilerParams(vmem_limit_bytes=40 << 20),
    )(present, gain, step_cov, update)

    total = suffix[0]
    size = lax.axis_size(AXES)
    by = 1
    while 2 * by < size:
        total = compose(total, moved(total, by), width)
        by *= 2
    near, far = moved(total, 1), moved(total, by + 1)
    carry = compose(near, far, width)[width:]

    mean, cov = pl.pallas_call(
        apply_kernel,
        grid=(length,),
        in_specs=[smem, stream, stream, fixed(steps, width), fixed(steps, width),
                  fixed(CHAINS, rows, width), fixed(width + PAD, width)],
        out_specs=[fixed(steps, width), stream],
        out_shape=[
            jax.ShapeDtypeStruct((steps, width), F32),
            jax.ShapeDtypeStruct((CHAINS, length, width, width), F32),
        ],
        scratch_shapes=[pltpu.VMEM((CHAINS, width + PAD, width), F32)],
        compiler_params=pltpu.CompilerParams(vmem_limit_bytes=40 << 20),
    )(present, gain, step_cov, update, pred_mean, suffix, carry)
    return mean, cov.reshape(steps, width, width)


def solution(mesh):
    placed = (P(AXES, None, None), P(AXES, None), P(AXES, None), P(AXES), P(AXES, None, None))
    return jax.shard_map(
        body,
        mesh=mesh,
        in_specs=placed,
        out_specs=(P(AXES, None), P(AXES, None, None)),
        check_vma=False,
    )
```

```python
import functools

import jax
import jax.numpy as jnp
from jax import lax
from jax.experimental import pallas as pl
from jax.experimental.pallas import tpu as pltpu
from jax.sharding import PartitionSpec as P

AXES = ("grp", "ta")
CHAINS = 16
GROUP = 16
PAD = 16
LIMIT = 60 << 20
F32, BF16 = jnp.float32, jnp.bfloat16


def halves(x):
    high = x.astype(BF16)
    low = (x - high.astype(F32)).astype(BF16)
    return high, low


def packed(x):
    return jnp.concatenate(halves(x), axis=1)


def weight_nt(g):
    high, low = halves(g)
    return jnp.concatenate(
        [jnp.concatenate([high, high], axis=1), jnp.concatenate([low, low], axis=1)], axis=0
    )


def weight_nn(g):
    row = packed(g)
    return jnp.concatenate([row, row], axis=0)


def diagonal_apart(g):
    on = lax.broadcasted_iota(jnp.int32, g.shape, 0) == lax.broadcasted_iota(jnp.int32, g.shape, 1)
    return jnp.sum(jnp.where(on, g, 0.0), axis=0, keepdims=True), jnp.where(on, 0.0, g)


def mul(x, w, dim, diagonal):
    out = lax.dot_general(packed(x), w, (((1,), (dim,)), ((), ())), preferred_element_type=F32)
    width = out.shape[1] // 2
    return out[:, :width] + out[:, width:] + x * diagonal


def begin(x, g, dim):
    diagonal, rest = diagonal_apart(g)
    w = weight_nt(rest) if dim else weight_nn(rest)
    return mul(x, w, dim, diagonal), w, diagonal


def finish(begun, dim, lead, cov, extra):
    y, w, diagonal = begun
    width = cov.shape[0]
    turned = y[lead : lead + width].T
    return y[:lead], mul(turned, w, dim, diagonal) + cov, y[lead + width :] + extra


def measured(pres_ref, upd_ref, row):
    here = pres_ref[row].astype(F32) * upd_ref[pl.ds(row, 1), :]
    return jnp.broadcast_to(here, (PAD, here.shape[1]))


def is_last():
    length = lax.axis_size("ta")
    at = lax.axis_index("grp") * length + lax.axis_index("ta")
    return at == lax.axis_size("grp") * length - 1


def summary_kernel(pres_ref, g_ref, q_ref, upd_ref, out_ref):
    t = pl.program_id(0)
    chains, length = CHAINS, pl.num_programs(0)
    width = g_ref.shape[-1]
    s = length - 1 - t
    keep = jnp.where(is_last(), 0.0, 1.0).astype(F32)

    @pl.when(t == 0)
    def _():
        for b in range(chains):
            g = g_ref[b, 0]
            if b == chains - 1:
                g = g * keep
            out_ref[b, :width] = g.T
            out_ref[b, width : 2 * width] = q_ref[b, 0]
            out_ref[b, 2 * width :] = measured(pres_ref, upd_ref, b * length + s)

    @pl.when(t > 0)
    def _():
        for group in range(0, chains, GROUP):
            members = range(group, group + GROUP)
            begun = [begin(out_ref[b], g_ref[b, 0], 1) for b in members]
            done = [
                finish(ahead, 1, width, q_ref[b, 0], measured(pres_ref, upd_ref, b * length + s))
                for b, ahead in zip(members, begun)
            ]
            for b, (lead, cov, d) in zip(members, done):
                out_ref[b, :width] = lead
                out_ref[b, width : 2 * width] = cov
                out_ref[b, 2 * width :] = d

    @pl.when(t == length - 1)
    def _():
        half = 1
        while half < chains:
            pairs = [
                (i, first + half)
                for first in range(0, chains, 2 * half)
                for i in range(first, first + half)
            ]
            begun = [begin(out_ref[later], out_ref[i, :width], 0) for i, later in pairs]
            done = [
                finish(ahead, 0, width, out_ref[i, width : 2 * width], out_ref[i, 2 * width :])
                for (i, later), ahead in zip(pairs, begun)
            ]
            for (i, later), (lead, cov, d) in zip(pairs, done):
                out_ref[i, :width] = lead
                out_ref[i, width : 2 * width] = cov
                out_ref[i, 2 * width :] = d
            half *= 2


def apply_kernel(pres_ref, g_ref, q_ref, upd_ref, pm_ref, suffix_ref, carry_ref, mean_ref, cov_ref, state):
    t = pl.program_id(0)
    chains, length = CHAINS, pl.num_programs(0)
    width = g_ref.shape[-1]
    s = length - 1 - t

    @pl.when(t == 0)
    def _():
        state[chains - 1] = jnp.where(is_last(), 0.0, carry_ref[...])
        begun = [begin(carry_ref[...], suffix_ref[b, :width], 0) for b in range(1, chains)]
        done = [
            finish(ahead, 0, 0, suffix_ref[b + 1, width : 2 * width], suffix_ref[b + 1, 2 * width :])
            for b, ahead in enumerate(begun)
        ]
        for b, (unused, cov, d) in enumerate(done):
            state[b, :width] = cov
            state[b, width:] = d

    keep = jnp.where(is_last() & (t == 0), 0.0, 1.0).astype(F32)
    for group in range(0, chains, GROUP):
        members = range(group, group + GROUP)
        begun = []
        for b in members:
            g = g_ref[b, 0]
            begun.append(begin(state[b], g * keep if b == chains - 1 else g, 1))
        done = [
            finish(ahead, 1, 0, q_ref[b, 0], measured(pres_ref, upd_ref, b * length + s))
            for b, ahead in zip(members, begun)
        ]
        for b, (unused, cov, d) in zip(members, done):
            row = b * length + s
            state[b, :width] = cov
            state[b, width:] = d
            cov_ref[b, 0] = cov
            mean_ref[pl.ds(row, 1), :] = pm_ref[pl.ds(row, 1), :] + d[:1]


def distances(size):
    by, rounds = 1, []
    while 2 * by < size:
        rounds.append(by)
        by *= 2
    return rounds, by + 1


def exchange_kernel(total_ref, carry_ref, held, got, far, sems):
    width = total_ref.shape[1]
    inner = lax.axis_size("ta")
    size = lax.axis_size("grp") * inner
    me = lax.axis_index("grp") * inner + lax.axis_index("ta")
    rounds, reach = distances(size)
    lead, rest = pl.ds(0, width), pl.ds(width, width + PAD)

    def device(offset):
        at = lax.rem(me + offset, size)
        return (at // inner, lax.rem(at, inner))

    barrier = pltpu.get_barrier_semaphore()
    offsets = sorted({o % size for by in rounds + [1, reach] for o in (by, -by)})
    for offset in offsets:
        pl.semaphore_signal(barrier, inc=1, device_id=device(offset), device_id_type=pl.DeviceIdType.MESH)
    pl.semaphore_wait(barrier, len(offsets))

    def send(source, target, sem, by):
        copy = pltpu.make_async_remote_copy(
            src_ref=source,
            dst_ref=target,
            send_sem=sems.at[sem, 0],
            recv_sem=sems.at[sem, 1],
            device_id=device(size - by),
            device_id_type=pl.DeviceIdType.MESH,
        )
        copy.start()
        return copy

    def received(copy, ref, by):
        copy.wait_recv()
        return jnp.where(me + by < size, ref[...], 0.0)

    hops = rounds + [1]
    last = len(rounds)
    held[0] = total_ref[...]
    first = send(held.at[0, lead], got.at[0, lead], 0, hops[0])
    second = send(held.at[0, rest], got.at[0, rest], 1, hops[0])
    sent = [first, second]
    for r, by in enumerate(rounds):
        turned = held[r, :width]
        diagonal, others = diagonal_apart(turned)
        w = weight_nn(others)
        joined = mul(received(first, got.at[r, lead], by), w, 0, diagonal)
        held[r + 1, :width] = joined
        first = send(held.at[r + 1, lead], got.at[r + 1, lead], 2 * r + 2, hops[r + 1])
        sent.append(first)
        y = mul(received(second, got.at[r, rest], by), w, 0, diagonal)
        held[r + 1, width : 2 * width] = mul(y[:width].T, w, 0, diagonal) + held[r, width : 2 * width]
        held[r + 1, 2 * width :] = y[width:] + held[r, 2 * width :]
        second = send(held.at[r + 1, rest], got.at[r + 1, rest], 2 * r + 3, hops[r + 1])
        sent.append(second)
        if r == last - 1:
            third = send(held.at[last, rest], far, 2 * last + 2, reach)
            sent.append(third)
    turned = received(first, got.at[last, lead], 1)
    diagonal, others = diagonal_apart(turned)
    w = weight_nn(others)
    y = mul(received(third, far, reach), w, 0, diagonal)
    near = received(second, got.at[last, rest], 1)
    carry_ref[:width] = mul(y[:width].T, w, 0, diagonal) + near[:width]
    carry_ref[width:] = y[width:] + near[width:]
    for copy in sent:
        copy.wait_send()


def body(gain, pred_mean, update, present, step_cov):
    steps, width = pred_mean.shape
    length = steps // CHAINS
    rows = 2 * width + PAD
    gain = gain.reshape(CHAINS, length, width, width)
    step_cov = step_cov.reshape(CHAINS, length, width, width)
    smem = pl.BlockSpec(memory_space=pltpu.SMEM)
    stream = pl.BlockSpec((CHAINS, 1, width, width), lambda t: (0, length - 1 - t, 0, 0))

    def fixed(*shape):
        return pl.BlockSpec(shape, lambda t: (0,) * len(shape))

    suffix = pl.pallas_call(
        summary_kernel,
        grid=(length,),
        in_specs=[smem, stream, stream, fixed(steps, width)],
        out_specs=fixed(CHAINS, rows, width),
        out_shape=jax.ShapeDtypeStruct((CHAINS, rows, width), F32),
        compiler_params=pltpu.CompilerParams(vmem_limit_bytes=LIMIT),
    )(present, gain, step_cov, update)

    rounds = len(distances(lax.axis_size(AXES))[0])
    carry = pl.pallas_call(
        exchange_kernel,
        grid=(1,),
        in_specs=[pl.BlockSpec((pl.squeezed, rows, width), lambda t: (0, 0, 0))],
        out_specs=fixed(width + PAD, width),
        out_shape=jax.ShapeDtypeStruct((width + PAD, width), F32),
        scratch_shapes=[
            pltpu.VMEM((rounds + 1, rows, width), F32),
            pltpu.VMEM((rounds + 1, rows, width), F32),
            pltpu.VMEM((width + PAD, width), F32),
            pltpu.SemaphoreType.DMA((2 * rounds + 3, 2)),
        ],
        compiler_params=pltpu.CompilerParams(
            collective_id=0, has_side_effects=True, vmem_limit_bytes=LIMIT
        ),
    )(suffix)

    mean, cov = pl.pallas_call(
        apply_kernel,
        grid=(length,),
        in_specs=[smem, stream, stream, fixed(steps, width), fixed(steps, width),
                  fixed(CHAINS, rows, width), fixed(width + PAD, width)],
        out_specs=[fixed(steps, width), stream],
        out_shape=[
            jax.ShapeDtypeStruct((steps, width), F32),
            jax.ShapeDtypeStruct((CHAINS, length, width, width), F32),
        ],
        scratch_shapes=[pltpu.VMEM((CHAINS, width + PAD, width), F32)],
        compiler_params=pltpu.CompilerParams(vmem_limit_bytes=LIMIT),
    )(present, gain, step_cov, update, pred_mean, suffix, carry)
    return mean, cov.reshape(steps, width, width)


def solution(mesh):
    placed = (P(AXES, None, None), P(AXES, None), P(AXES, None), P(AXES), P(AXES, None, None))
    return jax.shard_map(
        body,
        mesh=mesh,
        in_specs=placed,
        out_specs=(P(AXES, None), P(AXES, None, None)),
        check_vma=False,
    )
```
